32 devices in a mesh: ka: 16 (over z, y, x), orb: 2 (over core).
Axes of the slice: x: 2, y: 2, z: 4, core: 2. Of those that a mesh axis runs over, the one named last changes fastest.
Arguments:
- coeffs: bfloat16 [32, 8192, 256], P('ka', 'orb'), may hold values from -0.62890625 to 0.62890625
- perturbation: bfloat16 [2, 64, 8, 128, 128], P(None, 'orb'), may hold values from -0.1875 to 0.1875
- columns: int32 [64, 8], P('orb'), may hold values from 0 to 63, as said below
- images: int32 [3, 64, 8], P(None, 'orb'), may hold values from -2 to 2
- kpoints: int32 [32], P('ka'), may hold values from 0 to 32767
- matching: int32 [2, 32], replicated, may hold values from 0 to 31, each once within a row
Outputs:
- elph: float32 [32, 2, 2, 128, 128], P('ka', None, None, 'orb')
The draws below stay inside these ranges and needn't reach their ends.
Inputs may be any that keep to these rules, and one draw needn't show every extreme that they name: `columns`: row block i names 8 distinct column blocks in increasing order, always including i itself, all within the 9 consecutive blocks centred on i, the run moved inward at the two ends of the orbital range. `matching`: each row is a permutation of the k-points.
All inputs are finite; a program needn't handle non-finite values.
Results may differ from the reference program's by a relative error of at most 0.0039.
Values may be sent and summed in bfloat16 or wider, within the bound.
No kernel may reach another device: no remote copies, remote signals or barrier semaphores. Data moves between devices by JAX's collectives and lax.ppermute only.
A program may use at most 256 MiB of HBM per device.

```python
import math
import jax
import jax.numpy as jnp
from jax import lax

NO = 8192
BLK = 128
NB = 128
NNZ = 8
HALO = 4
NQ = 2
KGRID = 32
KPTS = 32
NBLK = 64


def draw_columns(key, part):
    block_rows = jnp.arange(NO // BLK).astype(jnp.int32)
    window_start = jnp.clip(block_rows - HALO, 0, NO // BLK - 2 * HALO - 1)
    diagonal = block_rows - window_start
    dropped = jax.random.randint(key, (NO // BLK,), 0, 2 * HALO).astype(jnp.int32)
    dropped = dropped + (dropped >= diagonal).astype(jnp.int32)
    offsets = jnp.arange(2 * HALO).astype(jnp.int32)
    placed = offsets[None, :] + (offsets[None, :] >= dropped[:, None]).astype(jnp.int32)
    return (window_start[:, None] + placed).astype(jnp.int32)


def with_ends(result, stream_key, smallest, largest):
    spot = [jax.random.randint(jax.random.fold_in(stream_key, axis), (), 0, length) for axis, length in enumerate(result.shape)]
    main_axis = result.shape.index(max(result.shape))
    next_to = spot[:main_axis] + [(spot[main_axis] + 1) % result.shape[main_axis]] + spot[main_axis + 1:]
    return result.at[tuple(spot)].set(smallest).at[tuple(next_to)].set(largest)


def shard_levels(stream_key, extent, split, least, largest):
    level = 1.0
    for dim, shards_of in split:
        draws = jax.random.uniform(jax.random.fold_in(jax.random.fold_in(stream_key, 6), dim), (shards_of,), jnp.float32, least / len(split), largest / len(split))
        level = level * jnp.repeat(jnp.exp(draws), extent[dim] // shards_of).reshape((-1,) + (1,) * (len(extent) - 1 - dim))
    return level


def bell_draw(stream_key, extent, width, limit, shards=(), kind=jnp.bfloat16):
    result = width * jax.random.normal(stream_key, extent, jnp.float32)
    if shards:
        result = result * shard_levels(stream_key, extent, shards, -0.22, 0.18)
    return jnp.clip(result, -limit, limit).astype(kind)


def setup_inputs(seed: int = 0) -> dict:
    splits = jax.random.split(jax.random.key(seed), 7)
    coeffs = bell_draw(splits[0], (KPTS, NO, 2 * NB), (NO ** -0.25), 0.62890625, ((0, 16), (1, 2)))
    perturbation = bell_draw(splits[1], (NQ, NBLK, NNZ, BLK, BLK), (NNZ * BLK) ** -0.5, 0.1875, ((1, 2),))
    columns = draw_columns(jax.random.fold_in(splits[6], 71), 0)
    images = with_ends(jax.random.randint(splits[3], (3, NBLK, NNZ), -2, 3), jax.random.fold_in(splits[3], 1), -2, 2).astype(jnp.int32)
    kpoints = with_ends(jax.random.randint(splits[4], (KPTS,), 0, KGRID ** 3), jax.random.fold_in(splits[4], 1), 0, (KGRID ** 3) - 1).astype(jnp.int32)
    matching = jax.vmap(lambda own: jax.random.permutation(own, KPTS))(jax.random.split(splits[5], NQ)).reshape((NQ, KPTS)).astype(jnp.int32)
    return {"coeffs": coeffs, "perturbation": perturbation, "columns": columns, "images": images, "kpoints": kpoints, "matching": matching}


def phases(kpoints, images):
    first_coord = kpoints // (KGRID * KGRID)
    second_coord = (kpoints // KGRID) % KGRID
    third_coord = kpoints % KGRID
    turn_count = (first_coord[:, None, None] * images[0][None] + second_coord[:, None, None] * images[1][None] + third_coord[:, None, None] * images[2][None]) % KGRID
    angles = turn_count.astype(jnp.float32) * (2.0 * math.pi / KGRID)
    return jnp.cos(angles), jnp.sin(angles)


def reference(coeffs, perturbation, columns, images, kpoints, matching):
    cosine, sine_part = phases(kpoints, images)
    weights = perturbation.astype(jnp.float32)
    positions = jnp.arange(KPTS).astype(jnp.int32)

    def one_point(position):
        ket_slab = coeffs[position]
        blocks = ket_slab.reshape(NO // BLK, BLK, 2 * NB)[columns]
        real_part = blocks[..., :NB].astype(jnp.float32)
        imag_part = blocks[..., NB:].astype(jnp.float32)
        cos_k = cosine[position][:, :, None, None]
        sin_k = sine_part[position][:, :, None, None]
        phased = jnp.concatenate([cos_k * real_part - sin_k * imag_part, sin_k * real_part + cos_k * imag_part], axis=-1).astype(jnp.bfloat16)
        ket_image = jnp.einsum("qistu,isuc->qitc", weights, phased.astype(jnp.float32))
        ket_image = ket_image.reshape(NQ, NO, 2 * NB).astype(jnp.bfloat16)
        bra_slabs = coeffs[matching[:, position]]
        product = jnp.einsum("qrb,qrc->qbc", bra_slabs.astype(jnp.float32), ket_image.astype(jnp.float32))
        matrix_real = product[:, :NB, :NB] + product[:, NB:, NB:]
        matrix_imag = product[:, :NB, NB:] - product[:, NB:, :NB]
        return jnp.stack([matrix_real, matrix_imag], axis=1)

    return lax.map(one_point, positions)
```

```python
import functools
import math

import jax
import jax.numpy as jnp
from jax import lax
from jax.experimental import pallas as pl
from jax.experimental.pallas import tpu as pltpu
from jax.sharding import PartitionSpec as P

BLK = 128
HALO = 4
KGRID = 32
VMEM = 48 * 1024 * 1024


def phases(kpoints, images):
    first_coord = kpoints // (KGRID * KGRID)
    second_coord = kpoints // KGRID % KGRID
    third_coord = kpoints % KGRID
    turn_count = (
        first_coord[:, None, None] * images[0][None]
        + second_coord[:, None, None] * images[1][None]
        + third_coord[:, None, None] * images[2][None]
    ) % KGRID
    angles = turn_count.astype(jnp.float32) * (2.0 * math.pi / KGRID)
    return (jnp.cos(angles), jnp.sin(angles))


def image_kernel(columns, cosine, sine, ket_ref, weight_ref, out_ref):
    block = pl.program_id(0)
    momenta, _, slots, size, _ = weight_ref.shape
    points, _, width = ket_ref.shape
    bands = width // 2
    weights = jnp.concatenate(
        [
            jnp.concatenate([weight_ref[q, 0, s] for s in range(slots)], axis=1)
            for q in range(momenta)
        ],
        axis=0,
    )
    for point in range(points):
        parts = []
        for s in range(slots):
            start = pl.multiple_of(columns[block, s] * size, size)
            real = ket_ref[point, pl.ds(start, size), :bands].astype(jnp.float32)
            imag = ket_ref[point, pl.ds(start, size), bands:].astype(jnp.float32)
            c, d = cosine[point, block, s], sine[point, block, s]
            turned = jnp.concatenate([c * real - d * imag, d * real + c * imag], axis=1)
            parts.append(turned.astype(jnp.bfloat16))
        image = jnp.dot(
            weights, jnp.concatenate(parts, axis=0), preferred_element_type=jnp.float32
        )
        for q in range(momenta):
            out_ref[point, q] = image[q * size : (q + 1) * size].astype(out_ref.dtype)


def ket_images(columns, cosine, sine, kets, weights):
    momenta, blocks, slots, size, _ = weights.shape
    points, rows, width = kets.shape
    flops = 2 * points * momenta * blocks * slots * size * size * width
    return pl.pallas_call(
        image_kernel,
        grid_spec=pltpu.PrefetchScalarGridSpec(
            num_scalar_prefetch=3,
            grid=(blocks,),
            in_specs=[
                pl.BlockSpec((points, rows, width), lambda i, *_: (0, 0, 0)),
                pl.BlockSpec((momenta, 1, slots, size, size), lambda i, *_: (0, i, 0, 0, 0)),
            ],
            out_specs=pl.BlockSpec((points, momenta, size, width), lambda i, *_: (0, 0, i, 0)),
        ),
        out_shape=jax.ShapeDtypeStruct((points, momenta, blocks * size, width), jnp.bfloat16),
        compiler_params=pltpu.CompilerParams(vmem_limit_bytes=VMEM),
        cost_estimate=pl.CostEstimate(
            flops=flops, bytes_accessed=weights.size * 2 + kets.size * 4, transcendentals=0
        ),
        name="ket_images",
    )(columns, cosine, sine, kets, weights)


def product_kernel(groups, bras, choice, *refs):
    image_refs, bra_refs = refs[:groups], refs[groups : groups + bras]
    out_ref, image_buf, bra_buf, image_sem, bra_sem = refs[groups + bras :]
    pairs = choice.shape[0]
    per_group = pairs // groups
    halves, half = out_ref.shape[0], out_ref.shape[3]
    bands = halves * half

    @pl.loop(0, pairs)
    def _(pair):
        wanted = choice[pair]
        for number, ref in enumerate(bra_refs):

            @pl.when(wanted == number)
            def _():
                pltpu.make_async_copy(ref, bra_buf.at[pair], bra_sem.at[pair]).start()

    def image_copy(group):
        spot = pl.ds(group * per_group, per_group)
        return pltpu.make_async_copy(image_refs[group], image_buf.at[spot], image_sem.at[group])

    for group in range(groups):
        image_copy(group).start()
    for group in range(groups):
        image_copy(group).wait()

        @pl.loop(group * per_group, (group + 1) * per_group)
        def _(pair):
            pltpu.make_async_copy(bra_refs[0], bra_buf.at[pair], bra_sem.at[pair]).wait()
            value = lax.dot_general(
                bra_buf[pair],
                image_buf[pair],
                (((0,), (0,)), ((), ())),
                preferred_element_type=jnp.float32,
            )
            real = value[:bands, :bands] + value[bands:, bands:]
            imag = value[:bands, bands:] - value[bands:, :bands]
            for h in range(halves):
                out_ref[h, pair, 0] = real[h * half : (h + 1) * half]
                out_ref[h, pair, 1] = imag[h * half : (h + 1) * half]


def products(choice, images, bras, halves):
    groups = len(images)
    rows, width = bras[0].shape
    pairs = choice.shape[0]
    bands = width // 2
    images = [image.reshape(pairs // groups, rows, width) for image in images]
    return pl.pallas_call(
        functools.partial(product_kernel, groups, len(bras)),
        in_specs=[pl.BlockSpec(memory_space=pltpu.SMEM)]
        + [pl.BlockSpec(memory_space=pl.ANY)] * (groups + len(bras)),
        out_specs=pl.BlockSpec(memory_space=pltpu.VMEM),
        out_shape=jax.ShapeDtypeStruct((halves, pairs, 2, bands // halves, bands), jnp.float32),
        scratch_shapes=[
            pltpu.VMEM((pairs, rows, width), jnp.bfloat16),
            pltpu.VMEM((pairs, rows, width), jnp.bfloat16),
            pltpu.SemaphoreType.DMA((groups,)),
            pltpu.SemaphoreType.DMA((pairs,)),
        ],
        compiler_params=pltpu.CompilerParams(vmem_limit_bytes=VMEM),
        cost_estimate=pl.CostEstimate(
            flops=2 * pairs * rows * width * width,
            bytes_accessed=4 * pairs * rows * width,
            transcendentals=0,
        ),
        name="products",
    )(choice, *images, *bras)


def per_device(coeffs, perturbation, columns, images, kpoints, matching):
    n_ka, n_orb = lax.axis_size("ka"), lax.axis_size("orb")
    points, row_count, width = coeffs.shape
    block_count = row_count // BLK
    momenta = perturbation.shape[0]
    bits_of = lambda n: n.bit_length() - 1
    n_rows = min(n_ka, block_count // (2 * HALO))
    n_side = n_ka // n_rows
    share = n_rows // n_orb
    blocks = block_count // n_rows
    rows = blocks * BLK
    me, core = lax.axis_index("ka"), lax.axis_index("orb")
    z, side = me // n_side, me % n_side

    def flat(zi, gi, ci):
        return (zi * n_side + gi) * n_orb + ci

    every = [(zi, gi, ci) for zi in range(n_rows) for gi in range(n_side) for ci in range(n_orb)]

    def send(x, to):
        moves = [(flat(*spot), to(*spot)) for spot in every]
        return lax.ppermute(x, ("ka", "orb"), [(a, flat(*b)) for a, b in moves if b is not None])

    def on_core(x, d):
        return send(x, lambda zi, gi, ci: (zi, gi, (ci + d) % n_orb))

    def across_rows(x, s):
        return send(x, lambda zi, gi, ci: (zi ^ s, gi, ci))

    def across_side(x, bit):
        return send(x, lambda zi, gi, ci: (zi, gi ^ (1 << bit), ci))

    def along(x, step):
        def to(zi, gi, ci):
            spot = zi * n_orb + ci + step
            return (spot // n_orb, gi, spot % n_orb) if 0 <= spot < n_rows * n_orb else None

        return send(x, to)

    def pick(x, index, axis):
        return lax.dynamic_index_in_dim(x, index, axis, keepdims=False)

    held = coeffs.reshape(points, share, n_orb, rows, width)
    mine = [pick(held, core, 2)]
    mine += [on_core(pick(held, (core + d) % n_orb, 2), d) for d in range(1, n_orb)]

    def slice_for(zi):
        source, index = zi // share, zi % share
        out = pick(mine[0], index, 1)
        for d in range(1, n_orb):
            out = jnp.where((core - source) % n_orb == d, pick(mine[d], index, 1), out)
        return out

    def own_rows(x, axis):
        def part(ci):
            index = (n_orb * z + ci) % n_rows
            return lax.dynamic_slice_in_dim(x, index * blocks, blocks, axis)

        source = (n_orb * z + core) // n_rows
        out = part(core)
        for d in range(1, n_orb):
            came = on_core(part((core + d) % n_orb), d)
            out = jnp.where((core - source) % n_orb == d, came, out)
        return out

    groups = [slice_for(z)]
    for s in range(1, n_rows):
        wanted = z ^ s
        if s > 2:
            token = groups[s - 2][0, 0, 0]
            wanted = wanted + (token != token).astype(wanted.dtype)
        groups.append(across_rows(slice_for(wanted), s))

    bits = list(range(bits_of(n_side)))
    bras = []
    for group in groups:
        have = []
        for point in range(points):
            found = {0: group[point]}
            turn = point % max(1, len(bits))
            for bit in bits[turn:] + bits[:turn]:
                found.update({p ^ (1 << bit): across_side(x, bit) for p, x in list(found.items())})
            have.append(found)
        bras += [have[point][p] for p in range(n_side) for point in range(points)]

    weights = own_rows(perturbation, 1)
    table = own_rows(jnp.concatenate([columns[None], images]), 1)
    local_columns = table[0] - (n_orb * z + core) * blocks + HALO
    reach = HALO * BLK

    def towards(s, step, start):
        edge = core == (n_orb - 1 if step > 0 else 0)
        out = groups[s][:, start : start + reach]
        for x in sorted({a ^ (a + 1) for a in range(n_rows - 1)}):
            other = groups[s ^ x][:, start : start + reach]
            out = jnp.where(edge & ((z ^ (z + step)) == x), other, out)
        return out

    ket_list, choices = [], []
    for s, group in enumerate(groups):
        before = along(towards(s, 1, rows - reach), 1)
        after = along(towards(s, -1, 0), -1)
        kets = jnp.concatenate([before, group, after], axis=1)
        k_here = kpoints if s == 0 else across_rows(kpoints, s)
        cosine, sine = phases(k_here, table[1:])
        ket_list.append(ket_images(local_columns, cosine, sine, kets, weights))
        first = ((z ^ s) * n_side + side) * points
        found = lax.dynamic_slice_in_dim(matching, first, points, 1).T
        owner = found // points
        number = ((owner // n_side) ^ z) * n_side + ((owner % n_side) ^ side)
        choices.append((number * points + found % points).reshape(-1))

    value = products(jnp.concatenate(choices), ket_list, bras, n_orb)
    total = pick(value, core, 0)
    for d in range(1, n_orb):
        total = total + on_core(pick(value, (core + d) % n_orb, 0), d)
    total = total.reshape(n_rows, points, momenta, *total.shape[1:])
    out = total[0]
    for s in range(1, n_rows):
        out = out + across_rows(total[s], s)
    return out


def solution(mesh):
    in_specs = (
        P("ka", "orb", None),
        P(None, "orb", None, None, None),
        P("orb", None),
        P(None, "orb", None),
        P("ka"),
        P(),
    )
    out_specs = P("ka", None, None, "orb", None)
    return jax.shard_map(
        per_device, mesh=mesh, in_specs=in_specs, out_specs=out_specs, check_vma=False
    )
```

```python
import functools
import math

import jax
import jax.numpy as jnp
from jax import lax
from jax.experimental import pallas as pl
from jax.experimental.pallas import tpu as pltpu
from jax.sharding import PartitionSpec as P

BLK = 128
HALO = 4
KGRID = 32
VMEM = 48 * 1024 * 1024


def phases(kpoints, images):
    first_coord = kpoints // (KGRID * KGRID)
    second_coord = kpoints // KGRID % KGRID
    third_coord = kpoints % KGRID
    turn_count = (
        first_coord[:, None, None] * images[0][None]
        + second_coord[:, None, None] * images[1][None]
        + third_coord[:, None, None] * images[2][None]
    ) % KGRID
    angles = turn_count.astype(jnp.float32) * (2.0 * math.pi / KGRID)
    return (jnp.cos(angles), jnp.sin(angles))


def image_kernel(core, columns, cosine, sine, outer_ref, ket_ref, inner_ref, weight_ref, out_ref, all_ref):
    block = pl.program_id(0)
    momenta, _, slots, size, _ = weight_ref.shape
    points, rows, width = ket_ref.shape
    reach = outer_ref.shape[2]
    bands = width // 2

    @pl.when(block == 0)
    def _():
        all_ref[:, reach : reach + rows] = ket_ref[...]
        outer_at = pl.multiple_of(core[0] * (reach + rows), size)
        inner_at = pl.multiple_of((1 - core[0]) * (reach + rows), size)
        all_ref[:, pl.ds(outer_at, reach)] = outer_ref[0]
        all_ref[:, pl.ds(inner_at, reach)] = inner_ref[0]

    weights = jnp.concatenate(
        [
            jnp.concatenate([weight_ref[q, 0, s] for s in range(slots)], axis=1)
            for q in range(momenta)
        ],
        axis=0,
    )
    for point in range(points):
        parts = []
        for s in range(slots):
            start = pl.multiple_of(columns[block, s] * size, size)
            real = all_ref[point, pl.ds(start, size), :bands].astype(jnp.float32)
            imag = all_ref[point, pl.ds(start, size), bands:].astype(jnp.float32)
            c, d = cosine[point, block, s], sine[point, block, s]
            turned = jnp.concatenate([c * real - d * imag, d * real + c * imag], axis=1)
            parts.append(turned.astype(jnp.bfloat16))
        image = jnp.dot(
            weights, jnp.concatenate(parts, axis=0), preferred_element_type=jnp.float32
        )
        for q in range(momenta):
            out_ref[point, q] = image[q * size : (q + 1) * size].astype(out_ref.dtype)


def ket_images(core, columns, cosine, sine, outer, kets, inner, weights):
    momenta, blocks, slots, size, _ = weights.shape
    points, rows, width = kets.shape
    reach = outer[0].shape[2]
    flops = 2 * points * momenta * blocks * slots * size * size * width

    def end(place):
        return pl.BlockSpec((1, points, reach, width), lambda i, *_: (place, 0, 0, 0))

    return pl.pallas_call(
        image_kernel,
        grid_spec=pltpu.PrefetchScalarGridSpec(
            num_scalar_prefetch=4,
            grid=(blocks,),
            in_specs=[
                end(outer[1]),
                pl.BlockSpec((points, rows, width), lambda i, *_: (0, 0, 0)),
                end(inner[1]),
                pl.BlockSpec((momenta, 1, slots, size, size), lambda i, *_: (0, i, 0, 0, 0)),
            ],
            out_specs=pl.BlockSpec((points, momenta, size, width), lambda i, *_: (0, 0, i, 0)),
            scratch_shapes=[pltpu.VMEM((points, rows + 2 * reach, width), jnp.bfloat16)],
        ),
        out_shape=jax.ShapeDtypeStruct((points, momenta, blocks * size, width), jnp.bfloat16),
        compiler_params=pltpu.CompilerParams(vmem_limit_bytes=VMEM),
        cost_estimate=pl.CostEstimate(
            flops=flops, bytes_accessed=weights.size * 2 + kets.size * 4, transcendentals=0
        ),
        name="ket_images",
    )(core, columns, cosine, sine, outer[0], kets, inner[0], weights)


def product_kernel(groups, places, choice, *refs):
    image_refs, bra_refs = refs[:groups], refs[groups:-5]
    out_ref, image_buf, bra_buf, image_sem, bra_sem = refs[-5:]
    pairs = choice.shape[0]
    per_group = pairs // groups
    halves, half = out_ref.shape[0], out_ref.shape[3]
    bands = halves * half

    @pl.loop(0, pairs)
    def _(pair):
        wanted = choice[pair]
        for number, (array, point) in enumerate(places):

            @pl.when(wanted == number)
            def _():
                source = bra_refs[array].at[point]
                pltpu.make_async_copy(source, bra_buf.at[pair], bra_sem.at[pair]).start()

    def image_copy(group):
        spot = pl.ds(group * per_group, per_group)
        return pltpu.make_async_copy(image_refs[group], image_buf.at[spot], image_sem.at[group])

    for group in range(groups):
        image_copy(group).start()
    for group in range(groups):
        image_copy(group).wait()

        @pl.loop(group * per_group, (group + 1) * per_group)
        def _(pair):
            pltpu.make_async_copy(bra_refs[0].at[0], bra_buf.at[pair], bra_sem.at[pair]).wait()
            value = lax.dot_general(
                bra_buf[pair],
                image_buf[pair],
                (((0,), (0,)), ((), ())),
                preferred_element_type=jnp.float32,
            )
            real = value[:bands, :bands] + value[bands:, bands:]
            imag = value[:bands, bands:] - value[bands:, :bands]
            for h in range(halves):
                out_ref[h, pair, 0] = real[h * half : (h + 1) * half]
                out_ref[h, pair, 1] = imag[h * half : (h + 1) * half]


def products(choice, images, bras, places, halves):
    groups = len(images)
    _, rows, width = bras[0].shape
    pairs = choice.shape[0]
    bands = width // 2
    images = [image.reshape(pairs // groups, rows, width) for image in images]
    return pl.pallas_call(
        functools.partial(product_kernel, groups, places),
        in_specs=[pl.BlockSpec(memory_space=pltpu.SMEM)]
        + [pl.BlockSpec(memory_space=pl.ANY)] * (groups + len(bras)),
        out_specs=pl.BlockSpec(memory_space=pltpu.VMEM),
        out_shape=jax.ShapeDtypeStruct((halves, pairs, 2, bands // halves, bands), jnp.float32),
        scratch_shapes=[
            pltpu.VMEM((pairs, rows, width), jnp.bfloat16),
            pltpu.VMEM((pairs, rows, width), jnp.bfloat16),
            pltpu.SemaphoreType.DMA((groups,)),
            pltpu.SemaphoreType.DMA((pairs,)),
        ],
        compiler_params=pltpu.CompilerParams(vmem_limit_bytes=VMEM),
        cost_estimate=pl.CostEstimate(
            flops=2 * pairs * rows * width * width,
            bytes_accessed=4 * pairs * rows * width,
            transcendentals=0,
        ),
        name="products",
    )(choice, *images, *bras)


def per_device(coeffs, perturbation, columns, images, kpoints, matching):
    n_ka, n_orb = lax.axis_size("ka"), lax.axis_size("orb")
    points, row_count, width = coeffs.shape
    block_count = row_count // BLK
    momenta = perturbation.shape[0]
    bits_of = lambda n: n.bit_length() - 1
    n_rows = min(n_ka, block_count // (2 * HALO))
    n_side = n_ka // n_rows
    blocks = block_count // n_rows
    rows = blocks * BLK
    me, core = lax.axis_index("ka"), lax.axis_index("orb")
    z, side = me // n_side, me % n_side

    def flat(zi, gi, ci):
        return (zi * n_side + gi) * n_orb + ci

    every = [(zi, gi, ci) for zi in range(n_rows) for gi in range(n_side) for ci in range(n_orb)]

    def send(x, to):
        moves = [(flat(*spot), to(*spot)) for spot in every]
        return lax.ppermute(x, ("ka", "orb"), [(a, flat(*b)) for a, b in moves if b is not None])

    def on_core(x, d):
        return send(x, lambda zi, gi, ci: (zi, gi, (ci + d) % n_orb))

    def across_rows(x, s):
        return send(x, lambda zi, gi, ci: (zi ^ s, gi, ci))

    def across_side(x, bit):
        return send(x, lambda zi, gi, ci: (zi, gi ^ (1 << bit), ci))

    def pick(x, index, axis):
        return lax.dynamic_index_in_dim(x, index, axis, keepdims=False)

    def after(x, *arrived):
        return lax.optimization_barrier((x, *arrived))[0] if arrived else x

    held = coeffs.reshape(points, n_rows, rows, width)

    def group_part(s, first, count, *arrived):
        target = z ^ s
        came = []
        source = after(held, *arrived)
        for ci in range(n_orb):
            part = pick(source[first : first + count], (n_orb * target + ci) % n_rows, 1)

            def to(zi, gi, cj, ci=ci):
                zt = zi ^ s
                return (zt, gi, ci) if (n_orb * zt + ci) // n_rows == cj else None

            came.append(send(part, to))
        return came

    def settle(came, *arrived):
        out = after(came[0], *arrived)
        for ci in range(1, n_orb):
            out = jnp.where(core == ci, came[ci], out)
        return out

    def own_group():
        source = (n_orb * z + core) // n_rows
        out = pick(held, (n_orb * z + core) % n_rows, 1)
        for d in range(1, n_orb):
            index = (n_orb * z + (core + d) % n_orb) % n_rows
            came = on_core(pick(held, index, 1), d)
            out = jnp.where((core - source) % n_orb == d, came, out)
        return out

    bits = list(range(bits_of(n_side)))

    def gather_side(group):
        near = [across_side(group, bit) for bit in bits]
        arrays = [group, *near]
        have, far = [], []
        for point in range(points):
            found = {0: (0, point), **{1 << bit: (1 + bit, point) for bit in bits}}
            for p in sorted(range(n_side), key=lambda n: n.bit_count()):
                if p not in found:
                    set_bits = [bit for bit in bits if p >> bit & 1]
                    bit = set_bits[-1 if point % 2 == 0 else 0]
                    array, place = found[p ^ (1 << bit)]
                    arrays.append(across_side(arrays[array][place : place + 1], bit))
                    far.append(arrays[-1])
                    found[p] = (len(arrays) - 1, 0)
            have.append(found)
        return arrays, have, near, far

    pieces = {}
    for s in range(1, n_rows):
        pieces[s] = group_part(s, 0, points, *([] if s < 3 else [pieces[s - 1][-1]]))
    groups, bras, places, near, far = [], [], [], [], []
    for s in range(n_rows):
        gates = (near[s - 1] if s > 0 else []) + (far[s - 2] if s > 1 else [])
        groups.append(settle(pieces[s], *gates) if s else own_group())
        arrays, have, came_near, came_far = gather_side(groups[s])
        for p in range(n_side):
            places += [(len(bras) + have[point][p][0], have[point][p][1]) for point in range(points)]
        bras += arrays
        near.append(came_near)
        far.append(came_far)

    def own_rows(x, axis, *arrived):
        def part(ci):
            index = (n_orb * z + ci) % n_rows
            return lax.dynamic_slice_in_dim(x, index * blocks, blocks, axis)

        x = after(x, *arrived)
        source = (n_orb * z + core) // n_rows
        out = part(core)
        for d in range(1, n_orb):
            came = on_core(part((core + d) % n_orb), d)
            out = jnp.where((core - source) % n_orb == d, came, out)
        return out

    weights = own_rows(perturbation, 1, *near[0])
    table = own_rows(jnp.concatenate([columns[None], images]), 1)
    local_columns = table[0] - (n_orb * z + core) * blocks + HALO
    reach = HALO * BLK
    lead = rows - reach

    def ends(members, start):
        return jnp.stack([lax.dynamic_slice_in_dim(x, start, reach, 1) for x in members])

    def outer_ends(wanted):
        step = jnp.where(core == 0, z ^ (z - 1), z ^ (z + 1))
        options = sorted({a ^ (a + 1) for a in range(n_rows - 1)})
        members = []
        for s in wanted:
            out = groups[s ^ options[0]]
            for x in options[1:]:
                out = jnp.where(step == x, groups[s ^ x], out)
            members.append(out)

        def to(zi, gi, ci):
            zt = zi + 2 * ci - 1
            return (zt, gi, 1 - ci) if 0 <= zt < n_rows else None

        return send(ends(members, core * lead), to)

    def inner_ends(wanted):
        return on_core(ends([groups[s] for s in wanted], (1 - core) * lead), 1)

    ket_list, choices = [None] * n_rows, []
    odd, even = list(range(1, n_rows, 2)), list(range(0, n_rows, 2))
    low, high = list(range(n_rows // 2)), list(range(n_rows // 2, n_rows))
    outer = {s: (x, i) for part in (odd, even) for x in [outer_ends(part)] for i, s in enumerate(part)}
    inner = {s: (x, i) for part in (low, high) for x in [inner_ends(part)] for i, s in enumerate(part)}
    for s in odd + even:
        k_here = kpoints if s == 0 else across_rows(kpoints, s)
        cosine, sine = phases(k_here, table[1:])
        ket_list[s] = ket_images(
            core[None], local_columns, cosine, sine, outer[s], groups[s], inner[s], weights
        )
    for s in range(n_rows):
        first = ((z ^ s) * n_side + side) * points
        found = lax.dynamic_slice_in_dim(matching, first, points, 1).T
        owner = found // points
        number = ((owner // n_side) ^ z) * n_side + ((owner % n_side) ^ side)
        choices.append((number * points + found % points).reshape(-1))

    value = products(jnp.concatenate(choices), ket_list, bras, places, n_orb)
    total = pick(value, core, 0)
    for d in range(1, n_orb):
        total = total + on_core(pick(value, (core + d) % n_orb, 0), d)
    total = total.reshape(n_rows, points, momenta, *total.shape[1:])
    out = total[0]
    for s in range(1, n_rows):
        out = out + across_rows(total[s], s)
    return out


def solution(mesh):
    in_specs = (
        P("ka", "orb", None),
        P(None, "orb", None, None, None),
        P("orb", None),
        P(None, "orb", None),
        P("ka"),
        P(),
    )
    out_specs = P("ka", None, None, "orb", None)
    return jax.shard_map(
        per_device, mesh=mesh, in_specs=in_specs, out_specs=out_specs, check_vma=False
    )
```

```python
import functools
import math

import jax
import jax.numpy as jnp
from jax import lax
from jax.experimental import pallas as pl
from jax.experimental.pallas import tpu as pltpu
from jax.sharding import PartitionSpec as P

BLK = 128
HALO = 4
KGRID = 32
VMEM = 48 * 1024 * 1024
KETCOST = 1
SPLIT = (2, 3)
PLAN = {
    "trade1": ["trade0"],
    "rows20": ["tables"],
    "rows21": ["rows20"],
    "rows30": ["rows21"],
    "second0": ["rows20"],
    "first1": ["first0", "second0", "rows21"],
    "weights": ["first0", "second0"],
    "first2": ["first1"],
    "second2": ["rows30"],
    "inner_low": ["second1"],
    "outer_odd": ["second1"],
    "inner_high": ["first2"],
    "outer_even": ["first2"],
    "first3": ["first2", "second1"],
    "second3": ["second2", "images_odd"],
    "rows31": ["rows30"],
}


def phases(kpoints, images):
    first_coord = kpoints // (KGRID * KGRID)
    second_coord = kpoints // KGRID % KGRID
    third_coord = kpoints % KGRID
    turn_count = (
        first_coord[:, None, None] * images[0][None]
        + second_coord[:, None, None] * images[1][None]
        + third_coord[:, None, None] * images[2][None]
    ) % KGRID
    angles = turn_count.astype(jnp.float32) * (2.0 * math.pi / KGRID)
    return (jnp.cos(angles), jnp.sin(angles))


def image_kernel(outer_places, inner_places, where, columns, cosine, sine, *refs):
    groups = len(outer_places)
    outer_refs, ket_refs, inner_refs = (refs[i * groups : (i + 1) * groups] for i in range(3))
    held_ref, sent_ref = refs[3 * groups : 3 * groups + 2]
    out_refs = refs[3 * groups + 2 : 4 * groups + 2]
    kets, weights, images, ket_sem, weight_sem, image_sem = refs[4 * groups + 2 :]
    points, rows, width = ket_refs[0].shape
    momenta, blocks, slots, size, _ = sent_ref.shape
    reach = outer_refs[0].shape[2]
    bands = width // 2
    core, is_home, first = where[0], where[1], where[2]

    def part(group, source, start, length, number):
        spot = pl.ds(pl.multiple_of(start, size), length)
        return pltpu.make_async_copy(source, kets.at[group, :, spot], ket_sem.at[group, number])

    parts = [
        [
            part(g, ket_refs[g], reach, rows, 0),
            part(g, outer_refs[g].at[outer_places[g]], core * (reach + rows), reach, 1),
            part(g, inner_refs[g].at[inner_places[g]], (1 - core) * (reach + rows), reach, 2),
        ]
        for g in range(groups)
    ]

    def weight_copy(block):
        return pltpu.make_async_copy(sent_ref.at[:, block], weights.at[:, block], weight_sem.at[block])

    def fetch_weights(count, start):
        @pl.when(is_home == 1)
        def _():
            for block in range(start, start + count):
                pltpu.make_async_copy(
                    held_ref.at[:, first + block], weights.at[:, block], weight_sem.at[block]
                ).start()

        @pl.when(is_home == 0)
        def _():
            for block in range(start, start + count):
                weight_copy(block).start()

    fetch_weights(1, 0)
    for copy in parts[0]:
        copy.start()
    fetch_weights(blocks - 1, 1)
    for copies in parts[1:]:
        for copy in copies:
            copy.start()

    def image_copy(group, block):
        spot = pl.ds(pl.multiple_of(block * size, size), size)
        return pltpu.make_async_copy(
            images.at[group, :, :, spot], out_refs[group].at[:, :, spot], image_sem.at[group, block]
        )

    for group in range(groups):
        for copy in parts[group]:
            copy.wait()

        @pl.loop(0, blocks)
        def _(block, group=group):
            if group == 0:
                weight_copy(block).wait()
            row = jnp.concatenate(
                [
                    jnp.concatenate([weights[q, block, s] for s in range(slots)], axis=1)
                    for q in range(momenta)
                ],
                axis=0,
            )
            spot = pl.ds(pl.multiple_of(block * size, size), size)
            for point in range(points):
                turned = []
                for s in range(slots):
                    start = pl.multiple_of(columns[block, s] * size, size)
                    real = kets[group, point, pl.ds(start, size), :bands].astype(jnp.float32)
                    imag = kets[group, point, pl.ds(start, size), bands:].astype(jnp.float32)
                    c, d = cosine[group * points + point, block, s], sine[group * points + point, block, s]
                    both = jnp.concatenate([c * real - d * imag, d * real + c * imag], axis=1)
                    turned.append(both.astype(jnp.bfloat16))
                image = jnp.dot(
                    row, jnp.concatenate(turned, axis=0), preferred_element_type=jnp.float32
                )
                for q in range(momenta):
                    images[group, point, q, spot] = image[q * size : (q + 1) * size].astype(images.dtype)
            image_copy(group, block).start()

    for group in range(groups):
        for block in range(blocks):
            image_copy(group, block).wait()


def ket_images(where, columns, cosine, sine, outer, kets, inner, held, sent):
    groups = len(kets)
    momenta, blocks, slots, size, _ = sent.shape
    points, rows, width = kets[0].shape
    reach = outer[0][0].shape[2]
    shape = (points, momenta, rows, width)
    places = [tuple(place for _, place in ends) for ends in (outer, inner)]
    return pl.pallas_call(
        functools.partial(image_kernel, *places),
        in_specs=[pl.BlockSpec(memory_space=pltpu.SMEM)] * 4
        + [pl.BlockSpec(memory_space=pl.ANY)] * (3 * groups + 2),
        out_specs=[pl.BlockSpec(memory_space=pl.ANY)] * groups,
        out_shape=[jax.ShapeDtypeStruct(shape, jnp.bfloat16)] * groups,
        scratch_shapes=[
            pltpu.VMEM((groups, points, rows + 2 * reach, width), jnp.bfloat16),
            pltpu.VMEM(sent.shape, jnp.bfloat16),
            pltpu.VMEM((groups, *shape), jnp.bfloat16),
            pltpu.SemaphoreType.DMA((groups, 3)),
            pltpu.SemaphoreType.DMA((blocks,)),
            pltpu.SemaphoreType.DMA((groups, blocks)),
        ],
        compiler_params=pltpu.CompilerParams(vmem_limit_bytes=VMEM),
        cost_estimate=pl.CostEstimate(
            flops=KETCOST * groups * 2 * points * momenta * blocks * slots * size * size * width,
            bytes_accessed=sent.size * 2 + groups * kets[0].size * 10,
            transcendentals=0,
        ),
        name="ket_images",
    )(where, columns, cosine, sine, *[x for x, _ in outer], *kets, *[x for x, _ in inner], held, sent)


def product_kernel(groups, places, choice, where, *refs):
    image_refs, bra_refs = refs[:groups], refs[groups:-6]
    kept_ref, given_ref, image_buf, bra_buf, image_sem, bra_sem = refs[-6:]
    pairs = choice.shape[0]
    per_group = pairs // groups
    half = kept_ref.shape[2]
    bands = 2 * half

    @pl.loop(0, pairs)
    def _(pair):
        wanted = choice[pair]
        for number, (array, point) in enumerate(places):

            @pl.when(wanted == number)
            def _():
                source = bra_refs[array].at[point]
                pltpu.make_async_copy(source, bra_buf.at[pair], bra_sem.at[pair]).start()

    def image_copy(pair):
        point, momentum = divmod(pair % per_group, image_refs[0].shape[1])
        source = image_refs[pair // per_group].at[point, momentum]
        return pltpu.make_async_copy(source, image_buf.at[pair], image_sem.at[pair])

    for pair in range(pairs):
        image_copy(pair).start()
    low = where[0] == 0
    for pair in range(pairs):
        image_copy(pair).wait()
        pltpu.make_async_copy(bra_refs[0].at[0], bra_buf.at[pair], bra_sem.at[pair]).wait()
        value = lax.dot_general(
            bra_buf[pair],
            image_buf[pair],
            (((0,), (0,)), ((), ())),
            preferred_element_type=jnp.float32,
        )
        real = value[:bands, :bands] + value[bands:, bands:]
        imag = value[:bands, bands:] - value[bands:, :bands]
        for part, x in enumerate((real, imag)):
            kept_ref[pair, part] = jnp.where(low, x[:half], x[half:])
            given_ref[pair, part] = jnp.where(low, x[half:], x[:half])


def products(choice, where, images, bras, places):
    groups = len(images)
    _, rows, width = bras[0].shape
    pairs = choice.shape[0]
    bands = width // 2
    half = jax.ShapeDtypeStruct((pairs, 2, bands // 2, bands), jnp.float32)
    return pl.pallas_call(
        functools.partial(product_kernel, groups, places),
        in_specs=[pl.BlockSpec(memory_space=pltpu.SMEM)] * 2
        + [pl.BlockSpec(memory_space=pl.ANY)] * (groups + len(bras)),
        out_specs=[pl.BlockSpec(memory_space=pltpu.VMEM)] * 2,
        out_shape=[half, half],
        scratch_shapes=[
            pltpu.VMEM((pairs, rows, width), jnp.bfloat16),
            pltpu.VMEM((pairs, rows, width), jnp.bfloat16),
            pltpu.SemaphoreType.DMA((pairs,)),
            pltpu.SemaphoreType.DMA((pairs,)),
        ],
        compiler_params=pltpu.CompilerParams(vmem_limit_bytes=VMEM),
        cost_estimate=pl.CostEstimate(
            flops=2 * pairs * rows * width * width,
            bytes_accessed=4 * pairs * rows * width,
            transcendentals=0,
        ),
        name="products",
    )(choice, where, *images, *bras)


def per_device(coeffs, perturbation, columns, images, kpoints, matching):
    n_ka, n_orb = lax.axis_size("ka"), lax.axis_size("orb")
    points, row_count, width = coeffs.shape
    block_count = row_count // BLK
    momenta = perturbation.shape[0]
    bits_of = lambda n: n.bit_length() - 1
    n_rows = min(n_ka, block_count // (2 * HALO))
    n_side = n_ka // n_rows
    blocks = block_count // n_rows
    share = n_rows // n_orb
    rows = blocks * BLK
    me, core = lax.axis_index("ka"), lax.axis_index("orb")
    z, side = me // n_side, me % n_side

    def flat(zi, gi, ci):
        return (zi * n_side + gi) * n_orb + ci

    every = [(zi, gi, ci) for zi in range(n_rows) for gi in range(n_side) for ci in range(n_orb)]

    def send(x, to):
        moves = [(flat(*spot), to(*spot)) for spot in every]
        return lax.ppermute(x, ("ka", "orb"), [(a, flat(*b)) for a, b in moves if b is not None])

    def on_core(x, d):
        return send(x, lambda zi, gi, ci: (zi, gi, (ci + d) % n_orb))

    def across_rows(x, s):
        return send(x, lambda zi, gi, ci: (zi ^ s, gi, ci))

    def across_side(x, bit):
        return send(x, lambda zi, gi, ci: (zi, gi ^ (1 << bit), ci))

    def pick(x, index, axis):
        return lax.dynamic_index_in_dim(x, index, axis, keepdims=False)

    def after(x, *arrived):
        return lax.optimization_barrier((x, *arrived))[0] if arrived else x

    done, todo = {}, []

    def step(name, needs, run):
        known = [other for other in PLAN.get(name, ()) if other not in needs]
        todo.append((name, [*needs, *known], known, run))

    def run_steps():
        while todo:
            for entry in todo:
                name, needs, known, run = entry
                if all(other in done for other in needs):
                    done[name] = run([x for other in known for x in jax.tree.leaves(done[other])])
                    todo.remove(entry)
                    break
            else:
                raise ValueError("circular plan")

    held = coeffs.reshape(points, share, n_orb, rows, width)
    is_home = core == z // share

    def trade(j, arrived):
        mine = pick(after(held, *arrived), (z ^ j) % share, 1)
        kept, given = pick(mine, core, 1), pick(mine, 1 - core, 1)
        came = on_core(given, 1)
        return lax.optimization_barrier((jnp.where(is_home, kept, came), jnp.where(is_home, came, kept)))

    for j in range(share):
        step(f"trade{j}", [], functools.partial(trade, j))

    def to_send(s):
        return done[f"trade{s % share}"][s // share]

    def tables(arrived):
        table = after(jnp.concatenate([columns[None], images]), *arrived)
        table = jnp.where(is_home, table, on_core(table, 1))
        table = lax.dynamic_slice_in_dim(table, (n_orb * z + core) % n_rows * blocks, blocks, 1)
        owned = after(kpoints[None], table)
        for bit in range(bits_of(n_rows)):
            owned = jnp.concatenate([owned, across_rows(owned, 1 << bit)])
        return table, owned

    step("tables", [], tables)

    first_mine = (n_orb * z + core) % n_rows * blocks

    def trade_weights(arrived):
        first_sent = (n_orb * z + 1 - core) % n_rows * blocks
        given = lax.dynamic_slice_in_dim(after(perturbation, *arrived), first_sent, blocks, 1)
        return on_core(given, 1)

    step("weights", [], trade_weights)

    for s in range(1, n_rows):
        size = 1 if s in SPLIT else points
        for i in range(points // size):

            def rows_from(arrived, s=s, i=i, size=size):
                return across_rows(after(to_send(s), *arrived)[i * size : (i + 1) * size], s)

            step(f"rows{s}{i}", [f"trade{s % share}"], rows_from)

        def whole(arrived, s=s, count=points // size):
            came = [done[f"rows{s}{i}"] for i in range(count)]
            return lax.optimization_barrier(jnp.concatenate(came) if count > 1 else came[0])

        step(f"group{s}", [f"rows{s}{i}" for i in range(points // size)], whole)
    step("group0", ["trade0"], lambda arrived: to_send(0))

    bits = list(range(bits_of(n_side)))
    bras, number_of = {}, {}

    def first_hops(s, arrived):
        group = after(done[f"group{s}"], *arrived)
        return [across_side(group, bit) for bit in bits]

    def second_hops(s, arrived):
        arrays = [done[f"group{s}"], *done[f"first{s}"]]
        came = []
        found = {(0, point): (0, point) for point in range(points)}
        found |= {(1 << bit, point): (1 + bit, point) for bit in bits for point in range(points)}
        for p in sorted(range(n_side), key=lambda n: n.bit_count()):
            for point in range(points):
                if (p, point) not in found:
                    bit = [bit for bit in bits if p >> bit & 1][-1 if point % 2 == 0 else 0]
                    array, place = found[p ^ (1 << bit), point]
                    came.append(across_side(after(arrays[array][place : place + 1], *arrived), bit))
                    found[p, point] = (len(arrays), 0)
                    arrays.append(came[-1])
        bras[s] = arrays
        number_of[s] = [found[p, point] for p in range(n_side) for point in range(points)]
        return came

    for s in range(n_rows):
        step(f"first{s}", [f"group{s}"], functools.partial(first_hops, s))
        step(f"second{s}", [f"first{s}"], functools.partial(second_hops, s))

    reach = HALO * BLK
    lead = rows - reach
    flips = sorted({a ^ (a + 1) for a in range(n_rows - 1)})

    def ends(members, start, arrived):
        return jnp.stack([lax.dynamic_slice_in_dim(after(x, *arrived), start, reach, 1) for x in members])

    def outer_ends(wanted, arrived):
        flip = jnp.where(core == 0, z ^ (z - 1), z ^ (z + 1))
        members = []
        for s in wanted:
            out = done[f"group{s ^ flips[0]}"]
            for x in flips[1:]:
                out = jnp.where(flip == x, done[f"group{s ^ x}"], out)
            members.append(out)

        def to(zi, gi, ci):
            zt = zi + 2 * ci - 1
            return (zt, gi, 1 - ci) if 0 <= zt < n_rows else None

        return send(ends(members, core * lead, arrived), to)

    def inner_ends(wanted, arrived):
        return on_core(ends([done[f"group{s}"] for s in wanted], (1 - core) * lead, arrived), 1)

    outer, inner = {}, {}
    parts = {"low": range(share), "high": range(share, n_rows), "odd": range(1, n_rows, 2), "even": range(0, n_rows, 2)}
    for name, part in parts.items():
        if name in ("low", "high"):
            needs = {f"group{s}" for s in part}
            step(f"inner_{name}", sorted(needs), functools.partial(inner_ends, part))
            inner |= {s: (f"inner_{name}", i) for i, s in enumerate(part)}
        else:
            needs = {f"group{s ^ x}" for s in part for x in flips}
            step(f"outer_{name}", sorted(needs), functools.partial(outer_ends, part))
            outer |= {s: (f"outer_{name}", i) for i, s in enumerate(part)}

    def images_of(part, arrived):
        table, owned = done["tables"]
        cosine, sine = phases(jnp.concatenate([owned[s] for s in part]), table[1:])
        return ket_images(
            jnp.stack([core, is_home.astype(core.dtype), first_mine]),
            table[0] - (n_orb * z + core) * blocks + HALO,
            cosine,
            sine,
            [(done[outer[s][0]], outer[s][1]) for s in part],
            [after(done[f"group{s}"], *arrived) for s in part],
            [(done[inner[s][0]], inner[s][1]) for s in part],
            perturbation,
            done["weights"],
        )

    for name in ("odd", "even"):
        needs = {need for s in parts[name] for need in (f"group{s}", outer[s][0], inner[s][0])}
        needs = sorted(needs) + ["tables", "weights"]
        step(f"images_{name}", needs, functools.partial(images_of, parts[name]))
    run_steps()

    places, arrays, choices = [], [], []
    for s in range(n_rows):
        places += [(len(arrays) + array, place) for array, place in number_of[s]]
        arrays += bras[s]
        first = ((z ^ s) * n_side + side) * points
        found = lax.dynamic_slice_in_dim(matching, first, points, 1)
        owner = found // points
        number = ((owner // n_side) ^ z) * n_side + ((owner % n_side) ^ side)
        choices.append((number * points + found % points).T.reshape(-1))

    kets = [None] * n_rows
    for name in ("odd", "even"):
        for s, x in zip(parts[name], done[f"images_{name}"]):
            kets[s] = x
    kept, given = products(jnp.concatenate(choices), core[None], kets, arrays, places)
    total = (kept + on_core(given, 1)).reshape(n_rows, points, momenta, *kept.shape[1:])
    out = total[0]
    for s in range(1, n_rows):
        out = out + across_rows(total[s].astype(jnp.bfloat16), s).astype(jnp.float32)
    return out


def solution(mesh):
    in_specs = (
        P("ka", "orb", None),
        P(None, "orb", None, None, None),
        P("orb", None),
        P(None, "orb", None),
        P("ka"),
        P(),
    )
    out_specs = P("ka", None, None, "orb", None)
    return jax.shard_map(
        per_device, mesh=mesh, in_specs=in_specs, out_specs=out_specs, check_vma=False
    )
```

```python
import functools
import math

import jax
import jax.numpy as jnp
from jax import lax
from jax.experimental import pallas as pl
from jax.experimental.pallas import tpu as pltpu
from jax.sharding import PartitionSpec as P

BLK = 128
HALO = 4
KGRID = 32
VMEM = 48 * 1024 * 1024
KETCOST = 1
SPLIT = (2, 3)
PLAN = {
    "trade1": ["trade0"],
    "rows20": ["tables"],
    "rows21": ["rows20"],
    "rows30": ["rows21"],
    "second0": ["rows20"],
    "first1": ["first0", "second0", "rows21"],
    "weights": ["first0", "second0"],
    "first2": ["first1"],
    "second2": ["rows30"],
    "inner_low": ["second1"],
    "outer_odd": ["second1"],
    "inner_high": ["first2"],
    "outer_even": ["first2"],
    "first3": ["first2", "second1"],
    "second3": ["second2", "images_odd"],
    "rows31": ["rows30"],
}


def phases(kpoints, images):
    first_coord = kpoints // (KGRID * KGRID)
    second_coord = kpoints // KGRID % KGRID
    third_coord = kpoints % KGRID
    turn_count = (
        first_coord[:, None, None] * images[0][None]
        + second_coord[:, None, None] * images[1][None]
        + third_coord[:, None, None] * images[2][None]
    ) % KGRID
    angles = turn_count.astype(jnp.float32) * (2.0 * math.pi / KGRID)
    return (jnp.cos(angles), jnp.sin(angles))


def image_kernel(outer_places, inner_places, where, columns, cosine, sine, *refs):
    groups = len(outer_places)
    outer_refs, ket_refs, inner_refs = (refs[i * groups : (i + 1) * groups] for i in range(3))
    held_ref, sent_ref = refs[3 * groups : 3 * groups + 2]
    out_refs = refs[3 * groups + 2 : 4 * groups + 2]
    kets, weights, images, ket_sem, weight_sem, image_sem = refs[4 * groups + 2 :]
    points, rows, width = ket_refs[0].shape
    momenta, blocks, slots, size, _ = sent_ref.shape
    reach = outer_refs[0].shape[2]
    bands = width // 2
    core, is_home, first = where[0], where[1], where[2]

    def part(group, source, start, length, number):
        spot = pl.ds(pl.multiple_of(start, size), length)
        return pltpu.make_async_copy(source, kets.at[group, :, spot], ket_sem.at[group, number])

    parts = [
        [
            part(g, ket_refs[g], reach, rows, 0),
            part(g, outer_refs[g].at[outer_places[g]], core * (reach + rows), reach, 1),
            part(g, inner_refs[g].at[inner_places[g]], (1 - core) * (reach + rows), reach, 2),
        ]
        for g in range(groups)
    ]

    def weight_copy(block):
        return pltpu.make_async_copy(sent_ref.at[:, block], weights.at[:, block], weight_sem.at[block])

    def fetch_weights(count, start):
        @pl.when(is_home == 1)
        def _():
            for block in range(start, start + count):
                pltpu.make_async_copy(
                    held_ref.at[:, first + block], weights.at[:, block], weight_sem.at[block]
                ).start()

        @pl.when(is_home == 0)
        def _():
            for block in range(start, start + count):
                weight_copy(block).start()

    fetch_weights(1, 0)
    for copy in parts[0]:
        copy.start()
    fetch_weights(blocks - 1, 1)
    for copies in parts[1:]:
        for copy in copies:
            copy.start()

    def image_copy(group, block):
        spot = pl.ds(pl.multiple_of(block * size, size), size)
        return pltpu.make_async_copy(
            images.at[group, :, :, spot], out_refs[group].at[:, :, spot], image_sem.at[group, block]
        )

    for group in range(groups):
        for copy in parts[group]:
            copy.wait()

        @pl.loop(0, blocks)
        def _(block, group=group):
            if group == 0:
                weight_copy(block).wait()
            row = jnp.concatenate(
                [
                    jnp.concatenate([weights[q, block, s] for s in range(slots)], axis=1)
                    for q in range(momenta)
                ],
                axis=0,
            )
            spot = pl.ds(pl.multiple_of(block * size, size), size)
            for point in range(points):
                turned = []
                for s in range(slots):
                    start = pl.multiple_of(columns[block, s] * size, size)
                    real = kets[group, point, pl.ds(start, size), :bands].astype(jnp.float32)
                    imag = kets[group, point, pl.ds(start, size), bands:].astype(jnp.float32)
                    c, d = cosine[group * points + point, block, s], sine[group * points + point, block, s]
                    both = jnp.concatenate([c * real - d * imag, d * real + c * imag], axis=1)
                    turned.append(both.astype(jnp.bfloat16))
                image = jnp.dot(
                    row, jnp.concatenate(turned, axis=0), preferred_element_type=jnp.float32
                )
                for q in range(momenta):
                    images[group, point, q, spot] = image[q * size : (q + 1) * size].astype(images.dtype)
            image_copy(group, block).start()

    for group in range(groups):
        for block in range(blocks):
            image_copy(group, block).wait()


def ket_images(where, columns, cosine, sine, outer, kets, inner, held, sent):
    groups = len(kets)
    momenta, blocks, slots, size, _ = sent.shape
    points, rows, width = kets[0].shape
    reach = outer[0][0].shape[2]
    shape = (points, momenta, rows, width)
    places = [tuple(place for _, place in ends) for ends in (outer, inner)]
    return pl.pallas_call(
        functools.partial(image_kernel, *places),
        in_specs=[pl.BlockSpec(memory_space=pltpu.SMEM)] * 4
        + [pl.BlockSpec(memory_space=pl.ANY)] * (3 * groups + 2),
        out_specs=[pl.BlockSpec(memory_space=pl.ANY)] * groups,
        out_shape=[jax.ShapeDtypeStruct(shape, jnp.bfloat16)] * groups,
        scratch_shapes=[
            pltpu.VMEM((groups, points, rows + 2 * reach, width), jnp.bfloat16),
            pltpu.VMEM(sent.shape, jnp.bfloat16),
            pltpu.VMEM((groups, *shape), jnp.bfloat16),
            pltpu.SemaphoreType.DMA((groups, 3)),
            pltpu.SemaphoreType.DMA((blocks,)),
            pltpu.SemaphoreType.DMA((groups, blocks)),
        ],
        compiler_params=pltpu.CompilerParams(vmem_limit_bytes=VMEM),
        cost_estimate=pl.CostEstimate(
            flops=KETCOST * groups * 2 * points * momenta * blocks * slots * size * size * width,
            bytes_accessed=sent.size * 2 + groups * kets[0].size * 10,
            transcendentals=0,
        ),
        name="ket_images",
    )(where, columns, cosine, sine, *[x for x, _ in outer], *kets, *[x for x, _ in inner], held, sent)


def product_kernel(groups, places, choice, where, *refs):
    image_refs, bra_refs = refs[:groups], refs[groups:-6]
    kept_ref, given_ref, image_buf, bra_buf, image_sem, bra_sem = refs[-6:]
    pairs = choice.shape[0]
    per_group = pairs // groups
    half = kept_ref.shape[2]
    bands = 2 * half

    def fetch(pair, low, high):
        if high - low == 1:
            array, point = places[low]
            source = bra_refs[array].at[point]
            pltpu.make_async_copy(source, bra_buf.at[pair], bra_sem.at[pair]).start()
            return
        middle = (low + high) // 2
        wanted = choice[pair]
        pl.when(wanted < middle)(lambda: fetch(pair, low, middle))
        pl.when(wanted >= middle)(lambda: fetch(pair, middle, high))

    def image_copy(pair):
        point, momentum = divmod(pair % per_group, image_refs[0].shape[1])
        source = image_refs[pair // per_group].at[point, momentum]
        return pltpu.make_async_copy(source, image_buf.at[pair], image_sem.at[pair])

    for pair in range(pairs):
        image_copy(pair).start()
        fetch(pair, 0, len(places))
    low = where[0] == 0
    for pair in range(pairs):
        image_copy(pair).wait()
        pltpu.make_async_copy(bra_refs[0].at[0], bra_buf.at[pair], bra_sem.at[pair]).wait()
        value = lax.dot_general(
            bra_buf[pair],
            image_buf[pair],
            (((0,), (0,)), ((), ())),
            preferred_element_type=jnp.float32,
        )
        real = value[:bands, :bands] + value[bands:, bands:]
        imag = value[:bands, bands:] - value[bands:, :bands]
        for part, x in enumerate((real, imag)):
            kept_ref[pair, part] = jnp.where(low, x[:half], x[half:])
            given_ref[pair, part] = jnp.where(low, x[half:], x[:half])


def products(choice, where, images, bras, places):
    groups = len(images)
    _, rows, width = bras[0].shape
    pairs = choice.shape[0]
    bands = width // 2
    half = jax.ShapeDtypeStruct((pairs, 2, bands // 2, bands), jnp.float32)
    return pl.pallas_call(
        functools.partial(product_kernel, groups, places),
        in_specs=[pl.BlockSpec(memory_space=pltpu.SMEM)] * 2
        + [pl.BlockSpec(memory_space=pl.ANY)] * (groups + len(bras)),
        out_specs=[pl.BlockSpec(memory_space=pltpu.VMEM)] * 2,
        out_shape=[half, half],
        scratch_shapes=[
            pltpu.VMEM((pairs, rows, width), jnp.bfloat16),
            pltpu.VMEM((pairs, rows, width), jnp.bfloat16),
            pltpu.SemaphoreType.DMA((pairs,)),
            pltpu.SemaphoreType.DMA((pairs,)),
        ],
        compiler_params=pltpu.CompilerParams(vmem_limit_bytes=VMEM),
        cost_estimate=pl.CostEstimate(
            flops=2 * pairs * rows * width * width,
            bytes_accessed=4 * pairs * rows * width,
            transcendentals=0,
        ),
        name="products",
    )(choice, where, *images, *bras)


def per_device(coeffs, perturbation, columns, images, kpoints, matching):
    n_ka, n_orb = lax.axis_size("ka"), lax.axis_size("orb")
    points, row_count, width = coeffs.shape
    block_count = row_count // BLK
    momenta = perturbation.shape[0]
    bits_of = lambda n: n.bit_length() - 1
    n_rows = min(n_ka, block_count // (2 * HALO))
    n_side = n_ka // n_rows
    blocks = block_count // n_rows
    share = n_rows // n_orb
    rows = blocks * BLK
    me, core = lax.axis_index("ka"), lax.axis_index("orb")
    z, side = me // n_side, me % n_side

    def flat(zi, gi, ci):
        return (zi * n_side + gi) * n_orb + ci

    every = [(zi, gi, ci) for zi in range(n_rows) for gi in range(n_side) for ci in range(n_orb)]

    def send(x, to):
        moves = [(flat(*spot), to(*spot)) for spot in every]
        return lax.ppermute(x, ("ka", "orb"), [(a, flat(*b)) for a, b in moves if b is not None])

    def on_core(x, d):
        return send(x, lambda zi, gi, ci: (zi, gi, (ci + d) % n_orb))

    def across_rows(x, s):
        return send(x, lambda zi, gi, ci: (zi ^ s, gi, ci))

    def across_side(x, bit):
        return send(x, lambda zi, gi, ci: (zi, gi ^ (1 << bit), ci))

    def pick(x, index, axis):
        return lax.dynamic_index_in_dim(x, index, axis, keepdims=False)

    def after(x, *arrived):
        return lax.optimization_barrier((x, *arrived))[0] if arrived else x

    done, todo = {}, []

    def step(name, needs, run):
        known = [other for other in PLAN.get(name, ()) if other not in needs]
        todo.append((name, [*needs, *known], known, run))

    def run_steps():
        while todo:
            for entry in todo:
                name, needs, known, run = entry
                if all(other in done for other in needs):
                    done[name] = run([x for other in known for x in jax.tree.leaves(done[other])])
                    todo.remove(entry)
                    break
            else:
                raise ValueError("circular plan")

    held = coeffs.reshape(points, share, n_orb, rows, width)
    is_home = core == z // share

    def trade(j, arrived):
        mine = pick(after(held, *arrived), (z ^ j) % share, 1)
        kept, given = pick(mine, core, 1), pick(mine, 1 - core, 1)
        came = on_core(given, 1)
        return lax.optimization_barrier((jnp.where(is_home, kept, came), jnp.where(is_home, came, kept)))

    for j in range(share):
        step(f"trade{j}", [], functools.partial(trade, j))

    def to_send(s):
        return done[f"trade{s % share}"][s // share]

    def tables(arrived):
        table = after(jnp.concatenate([columns[None], images]), *arrived)
        table = jnp.where(is_home, table, on_core(table, 1))
        table = lax.dynamic_slice_in_dim(table, (n_orb * z + core) % n_rows * blocks, blocks, 1)
        owned = after(kpoints[None], table)
        for bit in range(bits_of(n_rows)):
            owned = jnp.concatenate([owned, across_rows(owned, 1 << bit)])
        return table, owned

    step("tables", [], tables)

    first_mine = (n_orb * z + core) % n_rows * blocks

    def trade_weights(arrived):
        first_sent = (n_orb * z + 1 - core) % n_rows * blocks
        given = lax.dynamic_slice_in_dim(after(perturbation, *arrived), first_sent, blocks, 1)
        return on_core(given, 1)

    step("weights", [], trade_weights)

    for s in range(1, n_rows):
        size = 1 if s in SPLIT else points
        for i in range(points // size):

            def rows_from(arrived, s=s, i=i, size=size):
                return across_rows(after(to_send(s), *arrived)[i * size : (i + 1) * size], s)

            step(f"rows{s}{i}", [f"trade{s % share}"], rows_from)

        def whole(arrived, s=s, count=points // size):
            came = [done[f"rows{s}{i}"] for i in range(count)]
            return lax.optimization_barrier(jnp.concatenate(came) if count > 1 else came[0])

        step(f"group{s}", [f"rows{s}{i}" for i in range(points // size)], whole)
    step("group0", ["trade0"], lambda arrived: to_send(0))

    bits = list(range(bits_of(n_side)))
    bras, number_of = {}, {}

    def first_hops(s, arrived):
        group = after(done[f"group{s}"], *arrived)
        return [across_side(group, bit) for bit in bits]

    def second_hops(s, arrived):
        arrays = [done[f"group{s}"], *done[f"first{s}"]]
        came = []
        found = {(0, point): (0, point) for point in range(points)}
        found |= {(1 << bit, point): (1 + bit, point) for bit in bits for point in range(points)}
        for p in sorted(range(n_side), key=lambda n: n.bit_count()):
            for point in range(points):
                if (p, point) not in found:
                    bit = [bit for bit in bits if p >> bit & 1][-1 if point % 2 == 0 else 0]
                    array, place = found[p ^ (1 << bit), point]
                    came.append(across_side(after(arrays[array][place : place + 1], *arrived), bit))
                    found[p, point] = (len(arrays), 0)
                    arrays.append(came[-1])
        bras[s] = arrays
        number_of[s] = [found[p, point] for p in range(n_side) for point in range(points)]
        return came

    for s in range(n_rows):
        step(f"first{s}", [f"group{s}"], functools.partial(first_hops, s))
        step(f"second{s}", [f"first{s}"], functools.partial(second_hops, s))

    reach = HALO * BLK
    lead = rows - reach
    flips = sorted({a ^ (a + 1) for a in range(n_rows - 1)})

    def ends(members, start, arrived):
        return jnp.stack([lax.dynamic_slice_in_dim(after(x, *arrived), start, reach, 1) for x in members])

    def outer_ends(wanted, arrived):
        flip = jnp.where(core == 0, z ^ (z - 1), z ^ (z + 1))
        members = []
        for s in wanted:
            out = done[f"group{s ^ flips[0]}"]
            for x in flips[1:]:
                out = jnp.where(flip == x, done[f"group{s ^ x}"], out)
            members.append(out)

        def to(zi, gi, ci):
            zt = zi + 2 * ci - 1
            return (zt, gi, 1 - ci) if 0 <= zt < n_rows else None

        return send(ends(members, core * lead, arrived), to)

    def inner_ends(wanted, arrived):
        return on_core(ends([done[f"group{s}"] for s in wanted], (1 - core) * lead, arrived), 1)

    outer, inner = {}, {}
    parts = {"low": range(share), "high": range(share, n_rows), "odd": range(1, n_rows, 2), "even": range(0, n_rows, 2)}
    for name, part in parts.items():
        if name in ("low", "high"):
            needs = {f"group{s}" for s in part}
            step(f"inner_{name}", sorted(needs), functools.partial(inner_ends, part))
            inner |= {s: (f"inner_{name}", i) for i, s in enumerate(part)}
        else:
            needs = {f"group{s ^ x}" for s in part for x in flips}
            step(f"outer_{name}", sorted(needs), functools.partial(outer_ends, part))
            outer |= {s: (f"outer_{name}", i) for i, s in enumerate(part)}

    def images_of(part, arrived):
        table, owned = done["tables"]
        cosine, sine = phases(jnp.concatenate([owned[s] for s in part]), table[1:])
        return ket_images(
            jnp.stack([core, is_home.astype(core.dtype), first_mine]),
            table[0] - (n_orb * z + core) * blocks + HALO,
            cosine,
            sine,
            [(done[outer[s][0]], outer[s][1]) for s in part],
            [after(done[f"group{s}"], *arrived) for s in part],
            [(done[inner[s][0]], inner[s][1]) for s in part],
            perturbation,
            done["weights"],
        )

    for name in ("odd", "even"):
        needs = {need for s in parts[name] for need in (f"group{s}", outer[s][0], inner[s][0])}
        needs = sorted(needs) + ["tables", "weights"]
        step(f"images_{name}", needs, functools.partial(images_of, parts[name]))
    run_steps()

    places, arrays, choices = [], [], []
    for s in range(n_rows):
        places += [(len(arrays) + array, place) for array, place in number_of[s]]
        arrays += bras[s]
        first = ((z ^ s) * n_side + side) * points
        found = lax.dynamic_slice_in_dim(matching, first, points, 1)
        owner = found // points
        number = ((owner // n_side) ^ z) * n_side + ((owner % n_side) ^ side)
        choices.append((number * points + found % points).T.reshape(-1))

    kets = [None] * n_rows
    for name in ("odd", "even"):
        for s, x in zip(parts[name], done[f"images_{name}"]):
            kets[s] = x
    kept, given = products(jnp.concatenate(choices), core[None], kets, arrays, places)
    total = (kept + on_core(given, 1)).reshape(n_rows, points, momenta, *kept.shape[1:])
    out = total[0]
    for s in range(1, n_rows):
        out = out + across_rows(total[s].astype(jnp.bfloat16), s).astype(jnp.float32)
    return out


def solution(mesh):
    in_specs = (
        P("ka", "orb", None),
        P(None, "orb", None, None, None),
        P("orb", None),
        P(None, "orb", None),
        P("ka"),
        P(),
    )
    out_specs = P("ka", None, None, "orb", None)
    return jax.shard_map(
        per_device, mesh=mesh, in_specs=in_specs, out_specs=out_specs, check_vma=False
    )
```

```python
import functools
import math

import jax
import jax.numpy as jnp
from jax import lax
from jax.experimental import pallas as pl
from jax.experimental.pallas import tpu as pltpu
from jax.sharding import PartitionSpec as P

BLK = 128
HALO = 4
KGRID = 32
VMEM = 48 * 1024 * 1024
KETCOST = 1
SPLIT = (2, 3)
PLAN = {
    "trade1": ["trade0"],
    "rows20": ["tables"],
    "rows21": ["rows20"],
    "rows30": ["rows21"],
    "second0": ["rows20"],
    "first1": ["first0", "second0", "rows21"],
    "weights": ["first0", "second0"],
    "first2": ["first1"],
    "second2": ["rows30"],
    "inner_low": ["second1"],
    "outer_odd": ["second1"],
    "inner_high": ["first2"],
    "outer_even": ["first2"],
    "first3": ["first2", "second1"],
    "second3": ["second2", "images_odd"],
    "rows31": ["rows30"],
}


def phases(kpoints, images):
    first_coord = kpoints // (KGRID * KGRID)
    second_coord = kpoints // KGRID % KGRID
    third_coord = kpoints % KGRID
    turn_count = (
        first_coord[:, None, None] * images[0][None]
        + second_coord[:, None, None] * images[1][None]
        + third_coord[:, None, None] * images[2][None]
    ) % KGRID
    angles = turn_count.astype(jnp.float32) * (2.0 * math.pi / KGRID)
    return (jnp.cos(angles), jnp.sin(angles))


def image_kernel(outer_places, inner_places, where, columns, cosine, sine, *refs):
    groups = len(outer_places)
    outer_refs, ket_refs, inner_refs = (refs[i * groups : (i + 1) * groups] for i in range(3))
    held_ref, sent_ref = refs[3 * groups : 3 * groups + 2]
    out_refs = refs[3 * groups + 2 : 4 * groups + 2]
    kets, weights, images, ket_sem, weight_sem, image_sem = refs[4 * groups + 2 :]
    points, rows, width = ket_refs[0].shape
    momenta, blocks, slots, size, _ = sent_ref.shape
    reach = outer_refs[0].shape[2]
    bands = width // 2
    core, is_home, first = where[0], where[1], where[2]

    def part(group, source, start, length, number):
        spot = pl.ds(pl.multiple_of(start, size), length)
        return pltpu.make_async_copy(source, kets.at[group, :, spot], ket_sem.at[group, number])

    parts = [
        [
            part(g, ket_refs[g], reach, rows, 0),
            part(g, outer_refs[g].at[outer_places[g]], core * (reach + rows), reach, 1),
            part(g, inner_refs[g].at[inner_places[g]], (1 - core) * (reach + rows), reach, 2),
        ]
        for g in range(groups)
    ]

    def weight_copy(block):
        return pltpu.make_async_copy(sent_ref.at[:, block], weights.at[:, block], weight_sem.at[block])

    def fetch_weights(count, start):
        @pl.when(is_home == 1)
        def _():
            for block in range(start, start + count):
                pltpu.make_async_copy(
                    held_ref.at[:, first + block], weights.at[:, block], weight_sem.at[block]
                ).start()

        @pl.when(is_home == 0)
        def _():
            for block in range(start, start + count):
                weight_copy(block).start()

    fetch_weights(1, 0)
    for copy in parts[0]:
        copy.start()
    fetch_weights(blocks - 1, 1)
    for copies in parts[1:]:
        for copy in copies:
            copy.start()

    def image_copy(group, block):
        spot = pl.ds(pl.multiple_of(block * size, size), size)
        return pltpu.make_async_copy(
            images.at[group, :, :, spot], out_refs[group].at[:, :, spot], image_sem.at[group, block]
        )

    for group in range(groups):
        for copy in parts[group]:
            copy.wait()

        @pl.loop(0, blocks)
        def _(block, group=group):
            if group == 0:
                weight_copy(block).wait()
            row = jnp.concatenate(
                [
                    jnp.concatenate([weights[q, block, s] for s in range(slots)], axis=1)
                    for q in range(momenta)
                ],
                axis=0,
            )
            spot = pl.ds(pl.multiple_of(block * size, size), size)
            for point in range(points):
                turned = []
                for s in range(slots):
                    start = pl.multiple_of(columns[block, s] * size, size)
                    real = kets[group, point, pl.ds(start, size), :bands].astype(jnp.float32)
                    imag = kets[group, point, pl.ds(start, size), bands:].astype(jnp.float32)
                    c, d = cosine[group * points + point, block, s], sine[group * points + point, block, s]
                    both = jnp.concatenate([c * real - d * imag, d * real + c * imag], axis=1)
                    turned.append(both.astype(jnp.bfloat16))
                image = jnp.dot(
                    row, jnp.concatenate(turned, axis=0), preferred_element_type=jnp.float32
                )
                for q in range(momenta):
                    images[group, point, q, spot] = image[q * size : (q + 1) * size].astype(images.dtype)
            image_copy(group, block).start()

    for group in range(groups):
        for block in range(blocks):
            image_copy(group, block).wait()


def ket_images(where, columns, cosine, sine, outer, kets, inner, held, sent):
    groups = len(kets)
    momenta, blocks, slots, size, _ = sent.shape
    points, rows, width = kets[0].shape
    reach = outer[0][0].shape[2]
    shape = (points, momenta, rows, width)
    places = [tuple(place for _, place in ends) for ends in (outer, inner)]
    return pl.pallas_call(
        functools.partial(image_kernel, *places),
        in_specs=[pl.BlockSpec(memory_space=pltpu.SMEM)] * 4
        + [pl.BlockSpec(memory_space=pl.ANY)] * (3 * groups + 2),
        out_specs=[pl.BlockSpec(memory_space=pl.ANY)] * groups,
        out_shape=[jax.ShapeDtypeStruct(shape, jnp.bfloat16)] * groups,
        scratch_shapes=[
            pltpu.VMEM((groups, points, rows + 2 * reach, width), jnp.bfloat16),
            pltpu.VMEM(sent.shape, jnp.bfloat16),
            pltpu.VMEM((groups, *shape), jnp.bfloat16),
            pltpu.SemaphoreType.DMA((groups, 3)),
            pltpu.SemaphoreType.DMA((blocks,)),
            pltpu.SemaphoreType.DMA((groups, blocks)),
        ],
        compiler_params=pltpu.CompilerParams(vmem_limit_bytes=VMEM),
        cost_estimate=pl.CostEstimate(
            flops=KETCOST * groups * 2 * points * momenta * blocks * slots * size * size * width,
            bytes_accessed=sent.size * 2 + groups * kets[0].size * 10,
            transcendentals=0,
        ),
        name="ket_images",
    )(where, columns, cosine, sine, *[x for x, _ in outer], *kets, *[x for x, _ in inner], held, sent)


def product_kernel(groups, places, choice, where, *refs):
    image_refs, bra_refs = refs[:groups], refs[groups:-6]
    kept_ref, given_ref, image_buf, bra_buf, image_sem, bra_sem = refs[-6:]
    pairs = choice.shape[0]
    per_group = pairs // groups
    half = kept_ref.shape[2]
    bands = 2 * half

    def fetch(pair, low, high):
        if high - low == 1:
            array, point = places[low]
            source = bra_refs[array].at[point]
            pltpu.make_async_copy(source, bra_buf.at[pair], bra_sem.at[pair]).start()
            return
        middle = (low + high) // 2
        wanted = choice[pair]
        pl.when(wanted < middle)(lambda: fetch(pair, low, middle))
        pl.when(wanted >= middle)(lambda: fetch(pair, middle, high))

    def image_copy(pair):
        point, momentum = divmod(pair % per_group, image_refs[0].shape[1])
        source = image_refs[pair // per_group].at[point, momentum]
        return pltpu.make_async_copy(source, image_buf.at[pair], image_sem.at[pair])

    for pair in range(pairs):
        image_copy(pair).start()
        fetch(pair, 0, len(places))
    low = where[0] == 0
    for pair in range(pairs):
        image_copy(pair).wait()
        pltpu.make_async_copy(bra_refs[0].at[0], bra_buf.at[pair], bra_sem.at[pair]).wait()
        value = lax.dot_general(
            bra_buf[pair],
            image_buf[pair],
            (((0,), (0,)), ((), ())),
            preferred_element_type=jnp.float32,
        )
        real = value[:bands, :bands] + value[bands:, bands:]
        imag = value[:bands, bands:] - value[bands:, :bands]
        for part, x in enumerate((real, imag)):
            kept_ref[pair, part] = jnp.where(low, x[:half], x[half:])
            given_ref[pair, part] = jnp.where(low, x[half:], x[:half]).astype(given_ref.dtype)


def products(choice, where, images, bras, places):
    groups = len(images)
    _, rows, width = bras[0].shape
    pairs = choice.shape[0]
    bands = width // 2
    shape = (pairs, 2, bands // 2, bands)
    return pl.pallas_call(
        functools.partial(product_kernel, groups, places),
        in_specs=[pl.BlockSpec(memory_space=pltpu.SMEM)] * 2
        + [pl.BlockSpec(memory_space=pl.ANY)] * (groups + len(bras)),
        out_specs=[pl.BlockSpec(memory_space=pltpu.VMEM)] * 2,
        out_shape=[
            jax.ShapeDtypeStruct(shape, jnp.float32),
            jax.ShapeDtypeStruct(shape, jnp.bfloat16),
        ],
        scratch_shapes=[
            pltpu.VMEM((pairs, rows, width), jnp.bfloat16),
            pltpu.VMEM((pairs, rows, width), jnp.bfloat16),
            pltpu.SemaphoreType.DMA((pairs,)),
            pltpu.SemaphoreType.DMA((pairs,)),
        ],
        compiler_params=pltpu.CompilerParams(vmem_limit_bytes=VMEM),
        cost_estimate=pl.CostEstimate(
            flops=2 * pairs * rows * width * width,
            bytes_accessed=4 * pairs * rows * width,
            transcendentals=0,
        ),
        name="products",
    )(choice, where, *images, *bras)


def per_device(coeffs, perturbation, columns, images, kpoints, matching):
    n_ka, n_orb = lax.axis_size("ka"), lax.axis_size("orb")
    points, row_count, width = coeffs.shape
    block_count = row_count // BLK
    momenta = perturbation.shape[0]
    bits_of = lambda n: n.bit_length() - 1
    n_rows = min(n_ka, block_count // (2 * HALO))
    n_side = n_ka // n_rows
    blocks = block_count // n_rows
    share = n_rows // n_orb
    rows = blocks * BLK
    me, core = lax.axis_index("ka"), lax.axis_index("orb")
    z, side = me // n_side, me % n_side

    def flat(zi, gi, ci):
        return (zi * n_side + gi) * n_orb + ci

    every = [(zi, gi, ci) for zi in range(n_rows) for gi in range(n_side) for ci in range(n_orb)]

    def send(x, to):
        moves = [(flat(*spot), to(*spot)) for spot in every]
        return lax.ppermute(x, ("ka", "orb"), [(a, flat(*b)) for a, b in moves if b is not None])

    def on_core(x, d):
        return send(x, lambda zi, gi, ci: (zi, gi, (ci + d) % n_orb))

    def across_rows(x, s):
        return send(x, lambda zi, gi, ci: (zi ^ s, gi, ci))

    def across_side(x, bit):
        return send(x, lambda zi, gi, ci: (zi, gi ^ (1 << bit), ci))

    def pick(x, index, axis):
        return lax.dynamic_index_in_dim(x, index, axis, keepdims=False)

    def after(x, *arrived):
        return lax.optimization_barrier((x, *arrived))[0] if arrived else x

    done, todo = {}, []

    def step(name, needs, run):
        known = [other for other in PLAN.get(name, ()) if other not in needs]
        todo.append((name, [*needs, *known], known, run))

    def run_steps():
        while todo:
            for entry in todo:
                name, needs, known, run = entry
                if all(other in done for other in needs):
                    done[name] = run([x for other in known for x in jax.tree.leaves(done[other])])
                    todo.remove(entry)
                    break
            else:
                raise ValueError("circular plan")

    held = coeffs.reshape(points, share, n_orb, rows, width)
    is_home = core == z // share

    def trade(j, arrived):
        mine = pick(after(held, *arrived), (z ^ j) % share, 1)
        kept, given = pick(mine, core, 1), pick(mine, 1 - core, 1)
        came = on_core(given, 1)
        return lax.optimization_barrier((jnp.where(is_home, kept, came), jnp.where(is_home, came, kept)))

    for j in range(share):
        step(f"trade{j}", [], functools.partial(trade, j))

    def to_send(s):
        return done[f"trade{s % share}"][s // share]

    def tables(arrived):
        table = after(jnp.concatenate([columns[None], images]), *arrived)
        table = jnp.where(is_home, table, on_core(table, 1))
        table = lax.dynamic_slice_in_dim(table, (n_orb * z + core) % n_rows * blocks, blocks, 1)
        owned = after(kpoints[None], table)
        for bit in range(bits_of(n_rows)):
            owned = jnp.concatenate([owned, across_rows(owned, 1 << bit)])
        return table, owned

    step("tables", [], tables)

    first_mine = (n_orb * z + core) % n_rows * blocks

    def trade_weights(arrived):
        first_sent = (n_orb * z + 1 - core) % n_rows * blocks
        given = lax.dynamic_slice_in_dim(after(perturbation, *arrived), first_sent, blocks, 1)
        return on_core(given, 1)

    step("weights", [], trade_weights)

    for s in range(1, n_rows):
        size = 1 if s in SPLIT else points
        for i in range(points // size):

            def rows_from(arrived, s=s, i=i, size=size):
                return across_rows(after(to_send(s), *arrived)[i * size : (i + 1) * size], s)

            step(f"rows{s}{i}", [f"trade{s % share}"], rows_from)

        def whole(arrived, s=s, count=points // size):
            came = [done[f"rows{s}{i}"] for i in range(count)]
            return lax.optimization_barrier(jnp.concatenate(came) if count > 1 else came[0])

        step(f"group{s}", [f"rows{s}{i}" for i in range(points // size)], whole)
    step("group0", ["trade0"], lambda arrived: to_send(0))

    bits = list(range(bits_of(n_side)))
    bras, number_of = {}, {}

    def first_hops(s, arrived):
        group = after(done[f"group{s}"], *arrived)
        return [across_side(group, bit) for bit in bits]

    def second_hops(s, arrived):
        arrays = [done[f"group{s}"], *done[f"first{s}"]]
        came = []
        found = {(0, point): (0, point) for point in range(points)}
        found |= {(1 << bit, point): (1 + bit, point) for bit in bits for point in range(points)}
        for p in sorted(range(n_side), key=lambda n: n.bit_count()):
            for point in range(points):
                if (p, point) not in found:
                    bit = [bit for bit in bits if p >> bit & 1][-1 if point % 2 == 0 else 0]
                    array, place = found[p ^ (1 << bit), point]
                    came.append(across_side(after(arrays[array][place : place + 1], *arrived), bit))
                    found[p, point] = (len(arrays), 0)
                    arrays.append(came[-1])
        bras[s] = arrays
        number_of[s] = [found[p, point] for p in range(n_side) for point in range(points)]
        return came

    for s in range(n_rows):
        step(f"first{s}", [f"group{s}"], functools.partial(first_hops, s))
        step(f"second{s}", [f"first{s}"], functools.partial(second_hops, s))

    reach = HALO * BLK
    lead = rows - reach
    flips = sorted({a ^ (a + 1) for a in range(n_rows - 1)})

    def ends(members, start, arrived):
        return jnp.stack([lax.dynamic_slice_in_dim(after(x, *arrived), start, reach, 1) for x in members])

    def outer_ends(wanted, arrived):
        flip = jnp.where(core == 0, z ^ (z - 1), z ^ (z + 1))
        members = []
        for s in wanted:
            out = done[f"group{s ^ flips[0]}"]
            for x in flips[1:]:
                out = jnp.where(flip == x, done[f"group{s ^ x}"], out)
            members.append(out)

        def to(zi, gi, ci):
            zt = zi + 2 * ci - 1
            return (zt, gi, 1 - ci) if 0 <= zt < n_rows else None

        return send(ends(members, core * lead, arrived), to)

    def inner_ends(wanted, arrived):
        return on_core(ends([done[f"group{s}"] for s in wanted], (1 - core) * lead, arrived), 1)

    outer, inner = {}, {}
    parts = {"low": range(share), "high": range(share, n_rows), "odd": range(1, n_rows, 2), "even": range(0, n_rows, 2)}
    for name, part in parts.items():
        if name in ("low", "high"):
            needs = {f"group{s}" for s in part}
            step(f"inner_{name}", sorted(needs), functools.partial(inner_ends, part))
            inner |= {s: (f"inner_{name}", i) for i, s in enumerate(part)}
        else:
            needs = {f"group{s ^ x}" for s in part for x in flips}
            step(f"outer_{name}", sorted(needs), functools.partial(outer_ends, part))
            outer |= {s: (f"outer_{name}", i) for i, s in enumerate(part)}

    def images_of(part, arrived):
        table, owned = done["tables"]
        cosine, sine = phases(jnp.concatenate([owned[s] for s in part]), table[1:])
        return ket_images(
            jnp.stack([core, is_home.astype(core.dtype), first_mine]),
            table[0] - (n_orb * z + core) * blocks + HALO,
            cosine,
            sine,
            [(done[outer[s][0]], outer[s][1]) for s in part],
            [after(done[f"group{s}"], *arrived) for s in part],
            [(done[inner[s][0]], inner[s][1]) for s in part],
            perturbation,
            done["weights"],
        )

    for name in ("odd", "even"):
        needs = {need for s in parts[name] for need in (f"group{s}", outer[s][0], inner[s][0])}
        needs = sorted(needs) + ["tables", "weights"]
        step(f"images_{name}", needs, functools.partial(images_of, parts[name]))
    run_steps()

    places, arrays, choices = [], [], []
    for s in range(n_rows):
        places += [(len(arrays) + array, place) for array, place in number_of[s]]
        arrays += bras[s]
        first = ((z ^ s) * n_side + side) * points
        found = lax.dynamic_slice_in_dim(matching, first, points, 1)
        owner = found // points
        number = ((owner // n_side) ^ z) * n_side + ((owner % n_side) ^ side)
        choices.append((number * points + found % points).T.reshape(-1))

    kets = [None] * n_rows
    for name in ("odd", "even"):
        for s, x in zip(parts[name], done[f"images_{name}"]):
            kets[s] = x
    kept, given = products(jnp.concatenate(choices), core[None], kets, arrays, places)
    total = (kept + on_core(given, 1).astype(jnp.float32)).reshape(n_rows, points, momenta, *kept.shape[1:])
    out = total[0]
    for s in range(1, n_rows):
        out = out + across_rows(total[s].astype(jnp.bfloat16), s).astype(jnp.float32)
    return out


def solution(mesh):
    in_specs = (
        P("ka", "orb", None),
        P(None, "orb", None, None, None),
        P("orb", None),
        P(None, "orb", None),
        P("ka"),
        P(),
    )
    out_specs = P("ka", None, None, "orb", None)
    return jax.shard_map(
        per_device, mesh=mesh, in_specs=in_specs, out_specs=out_specs, check_vma=False
    )
```
